32 devices in a mesh: owner: 8 (over z, x), tensor: 4 (over y, core).
Axes of the slice: x: 2, y: 2, z: 4, core: 2. Of those that a mesh axis runs over, the one named last changes fastest.
Arguments:
- gradients: bfloat16 [40, 1536, 512], P(None, 'owner', 'tensor'), may hold values from -12 to 12
- moments: bfloat16 [40, 1536, 512], P(None, 'owner', 'tensor'), may hold values from -12 to 12
- stats: float32 [64, 512, 512], P(('owner', 'tensor')), may hold values from -1 to 11, as said below
- bases: float32 [64, 512, 512], P(('owner', 'tensor')), may hold values from -1 to 2
- second: bfloat16 [64, 1536, 512], P(('owner', 'tensor')), may hold values from 0.19921875 to 8
- owner_list: int32 [40], replicated, may hold values from 0 to 31, as said below
Outputs:
- new_moments: bfloat16 [40, 1536, 512], P(None, 'owner', 'tensor')
- update: bfloat16 [40, 1536, 512], P(None, 'owner', 'tensor')
- new_stats: float32 [64, 512, 512], P(('owner', 'tensor'))
- new_bases: float32 [64, 512, 512], P(('owner', 'tensor'))
- new_second: bfloat16 [64, 1536, 512], P(('owner', 'tensor'))
The draws below stay inside these ranges and needn't reach their ends.
Inputs may be any that keep to these rules, and one draw needn't show every extreme that they name: `owner_list`: no device owns more than 2 matrices, and at least one owns 2. `stats`: Symmetric.
All inputs are finite; a program needn't handle non-finite values.
Results may differ from the reference program's by a relative error of at most 0.0077.
Values may be sent and summed in bfloat16 or wider, within the bound.
A program may use at most 128 MiB of HBM per device.

```python
import math
import jax
import jax.numpy as jnp
from jax import lax

ROWS = 1536
COLS = 512
CAP = 2
NM = 40
SLOTS = 64
N_OWNER = 8
N_TENSOR = 4


def draw_owner_list(key, part):
    devices = N_OWNER * N_TENSOR
    chosen = jax.random.permutation(key, devices * CAP)[:NM]
    return (chosen // CAP).astype(jnp.int32)


def draw_stats(key, part):
    total = N_OWNER * N_TENSOR * CAP
    key_noise = jax.random.fold_in(key, 11)
    key_diag = jax.random.fold_in(key, 12)
    noise = jax.random.truncated_normal(key_noise, -4.0, 4.0, (total, COLS, COLS), jnp.float32)
    symmetric = (noise + jnp.swapaxes(noise, 1, 2)) * (0.45 / (1.4142135 * COLS ** 0.5))
    diag_vals = jax.random.uniform(key_diag, (total, COLS), jnp.float32, 1.0, 3.0)
    eye_mat = jnp.eye(COLS, dtype=jnp.float32)
    return symmetric + diag_vals[:, :, None] * eye_mat[None, :, :]


def draw_bases(key, part):
    total = N_OWNER * N_TENSOR * CAP
    key_noise = jax.random.fold_in(key, 21)
    noise = jax.random.truncated_normal(key_noise, -4.0, 4.0, (total, COLS, COLS), jnp.float32)
    eye_mat = jnp.eye(COLS, dtype=jnp.float32)
    return eye_mat[None, :, :] + noise * (0.3 / COLS ** 0.5)


def block_scale(own_key, shape, cuts, smallest, largest):
    def one(dim, blocks):
        heights = jax.random.uniform(jax.random.fold_in(jax.random.fold_in(own_key, 6), dim), (blocks,), jnp.float32, smallest / len(cuts), largest / len(cuts))
        return jnp.repeat(jnp.exp(heights), shape[dim] // blocks).reshape((-1,) + (1,) * (len(shape) - dim - 1))

    loudness = one(*cuts[0])
    for cut in cuts[1:]:
        loudness = loudness * one(*cut)
    return loudness


def centred(key, extent, deviation, most, shards=(), kind=jnp.bfloat16):
    entries = jax.random.normal(key, extent, jnp.float32) * deviation
    if len(shards) > 0:
        entries = block_scale(key, extent, shards, -0.22, 0.18) * entries
    return jnp.clip(entries, min=-most, max=most).astype(kind)


def setup_inputs(seed: int = 0) -> dict:
    key_list = jax.random.split(jax.random.key(seed), 7)
    return {
        "gradients": centred(key_list[0], (NM, ROWS, COLS), 2.0, 12.0, ((1, 8), (2, 4))),
        "moments": centred(key_list[1], (NM, ROWS, COLS), 2.0, 12.0, ((1, 8), (2, 4))),
        "stats": draw_stats(jax.random.fold_in(key_list[6], 71), 0),
        "bases": draw_bases(jax.random.fold_in(key_list[6], 71), 0),
        "second": jnp.clip(jnp.exp(math.log(8.0) - 3.6927934 * jax.random.uniform(key_list[4], (SLOTS, ROWS, COLS), jnp.float32) ** block_scale(key_list[4], (SLOTS, ROWS, COLS), ((0, 32),), -0.2, 0.2)), 0.19921875, 8.0).astype(jnp.bfloat16),
        "owner_list": draw_owner_list(jax.random.fold_in(key_list[6], 71), 0),
    }


def refine(iterate):
    for sweep in range(2):
        iter_b = iterate.astype(jnp.bfloat16)
        square = jnp.dot(iter_b.T, iter_b, preferred_element_type=jnp.float32).astype(jnp.bfloat16)
        iterate = 1.5 * iterate - 0.5 * jnp.dot(iter_b, square, preferred_element_type=jnp.float32)
    return iterate

def reference(gradients, moments, stats, bases, second, owner_list):
    slot_total = N_OWNER * N_TENSOR * CAP
    matrix_ids = jnp.arange(NM, dtype=jnp.int32)
    shared = owner_list[:, None] == owner_list[None, :]
    earlier = matrix_ids[:, None] < matrix_ids[None, :]
    position = lax.optimization_barrier(jnp.sum((shared & earlier).astype(jnp.int32), axis=0))
    slot_id = (owner_list * CAP + position).astype(jnp.int32)
    new_moments = (0.9 * moments.astype(jnp.float32) + 0.1 * gradients.astype(jnp.float32)).astype(jnp.bfloat16)

    def one_matrix(which):
        slot_now = slot_id[which]
        grad_mat = gradients[which]
        moment_mat = new_moments[which]
        stat_old = stats[slot_now]
        basis_old = bases[slot_now]
        second_old = second[slot_now].astype(jnp.float32)
        gram = jnp.dot(grad_mat.T, grad_mat, preferred_element_type=jnp.float32)
        stat_next = 0.95 * stat_old + 0.05 / ROWS * gram
        basis_b = basis_old.astype(jnp.bfloat16)
        rotated = jnp.dot(grad_mat, basis_b, preferred_element_type=jnp.float32)
        second_next = 0.95 * second_old + 0.05 * rotated * rotated
        moment_rot = jnp.dot(moment_mat, basis_b, preferred_element_type=jnp.float32)
        scaled = (moment_rot / (jnp.sqrt(second_next) + 1e-06)).astype(jnp.bfloat16)
        step_mat = jnp.dot(scaled, basis_b.T, preferred_element_type=jnp.float32).astype(jnp.bfloat16)
        power = jnp.dot(stat_next, basis_old, precision=lax.Precision.HIGHEST, preferred_element_type=jnp.float32)
        iterate = power / (2.0 * jnp.sqrt(COLS * jnp.mean(power * power) + 1e-06))
        return (step_mat, stat_next, refine(iterate), second_next.astype(jnp.bfloat16))
    steps_all, stats_all, bases_all, second_all = lax.map(one_matrix, matrix_ids)
    new_stats = jnp.zeros((slot_total, COLS, COLS), jnp.float32).at[slot_id].set(stats_all)
    new_bases = jnp.zeros((slot_total, COLS, COLS), jnp.float32).at[slot_id].set(bases_all)
    new_second = jnp.zeros((slot_total, ROWS, COLS), jnp.bfloat16).at[slot_id].set(second_all)
    return (new_moments, steps_all, new_stats, new_bases, new_second)
```

```python
import functools

import jax
import jax.numpy as jnp
from jax import lax
from jax.experimental import pallas as pl
from jax.experimental.pallas import tpu as pltpu
from jax.sharding import PartitionSpec as P

MESH = pl.DeviceIdType.MESH
F32 = jnp.float32
BF16 = jnp.bfloat16


def dot(a, b, ca, cb, precision=None):
    return lax.dot_general(
        a, b, (((ca,), (cb,)), ((), ())), precision=precision, preferred_element_type=F32
    )


def step_kernel(
    owners,
    tensors,
    which_ref,
    valid_ref,
    slot_ref,
    grads_hbm,
    moms_hbm,
    stats_hbm,
    bases_hbm,
    second_hbm,
    newm_out,
    update_out,
    stats_out,
    bases_out,
    second_out,
    grads,
    moms,
    stats,
    bases,
    second,
    basis_b,
    gram,
    send,
    got,
    steps,
    back,
    update,
    in_sem,
    out_sem,
    send_sem,
    got_sem,
    step_sem,
    back_sem,
):
    devices = owners * tensors
    matrices, rows, cols = grads.shape
    cap, full_cols = bases.shape[0], bases.shape[2]
    full_rows = owners * rows
    levels = 4
    across = owners // levels
    me_o, me_t = lax.axis_index("owner"), lax.axis_index("tensor")
    me = me_o * tensors + me_t
    level, column = me_o // across, me_o % across
    my_cols = pl.ds(pl.multiple_of(me_t * cols, cols), cols)

    def shift(s):
        q = s % levels
        by = jnp.where(q == 0, 2, jnp.where(q == 1, 1, jnp.where(q == 2, 3, 0)))
        return by, (s // levels + 1) % across

    def target(s):
        by_level, by_column = shift(s)
        return ((level + by_level) % levels) * across + (column + by_column) % across

    def source(s):
        by_level, by_column = shift(s)
        return ((level - by_level + levels) % levels) * across + (
            column - by_column + across
        ) % across

    loads = [
        pltpu.make_async_copy(src, dst, in_sem.at[i])
        for i, (src, dst) in enumerate(
            (
                (grads_hbm, grads),
                (moms_hbm, moms),
                (bases_hbm, bases),
                (second_hbm, second),
                (stats_hbm, stats),
            )
        )
    ]
    for load in loads:
        load.start()

    barrier = pltpu.get_barrier_semaphore()

    def greet(k, carry):
        pl.semaphore_signal(
            barrier,
            inc=1,
            device_id=(target(k // tensors), (me_t + k % tensors + 1) % tensors),
            device_id_type=MESH,
        )
        return carry

    lax.fori_loop(0, devices - 1, greet, 0)
    loads[0].wait()
    loads[1].wait()

    def moment(j, carry):
        moms[j] = (0.9 * moms[j].astype(F32) + 0.1 * grads[j].astype(F32)).astype(BF16)
        return carry

    lax.fori_loop(0, matrices, moment, 0)
    pl.semaphore_wait(barrier, devices - 1)

    def fill(k, device):
        for c in range(cap):
            which = which_ref[device * cap + c]
            send[k, c, 0] = grads[which]
            send[k, c, 1] = moms[which]

    def deal(k, carry):
        to, t = target(k // tensors), (me_t + k % tensors + 1) % tensors
        fill(k, to * tensors + t)
        pltpu.make_async_remote_copy(
            src_ref=send.at[k],
            dst_ref=got.at[me_o, :, :, :, my_cols],
            send_sem=send_sem,
            recv_sem=got_sem.at[me_o],
            device_id=(to, t),
            device_id_type=MESH,
        ).start()
        return carry

    lax.fori_loop(0, devices - 1, deal, 0)
    fill(devices - 1, me)
    pltpu.make_async_copy(
        send.at[devices - 1], got.at[me_o, :, :, :, my_cols], got_sem.at[me_o]
    ).start()
    newm_store = pltpu.make_async_copy(moms, newm_out, out_sem.at[0])
    newm_store.start()

    for load in loads[2:]:
        load.wait()
    for c in range(cap):
        basis_b[c] = bases[c].astype(BF16)
        gram[c] = jnp.zeros((full_cols, full_cols), F32)

    def work(s, carry):
        frm = source(s)
        pltpu.make_async_copy(got.at[frm], got.at[frm], got_sem.at[frm]).wait()

        def one(c, carry):
            grad, mom, basis = got[frm, c, 0], got[frm, c, 1], basis_b[c]
            gram[c] += dot(grad, grad, 0, 0)
            rotated = dot(grad, basis, 1, 0)
            following = 0.95 * second[c, frm].astype(F32) + 0.05 * rotated * rotated
            moment_rot = dot(mom, basis, 1, 0)
            scaled = (moment_rot / (jnp.sqrt(following) + 1e-06)).astype(BF16)
            steps[s, c] = dot(scaled, basis, 1, 1).astype(BF16)
            filled = valid_ref[me * cap + c] > 0
            second[c, frm] = jnp.where(filled, following, 0.0).astype(BF16)
            return carry

        lax.fori_loop(0, cap, one, 0)

        def give(i, carry):
            t = (me_t + i + 1) % tensors
            piece = steps.at[s, :, :, pl.ds(pl.multiple_of(t * cols, cols), cols)]

            @pl.when(s * tensors + i < devices - 1)
            def _():
                pltpu.make_async_remote_copy(
                    src_ref=piece,
                    dst_ref=back.at[me],
                    send_sem=step_sem,
                    recv_sem=back_sem,
                    device_id=(frm, t),
                    device_id_type=MESH,
                ).start()

            @pl.when(s * tensors + i == devices - 1)
            def _():
                pltpu.make_async_copy(piece, back.at[me], back_sem).start()

            return carry

        lax.fori_loop(0, tensors, give, 0)
        return carry

    lax.fori_loop(0, owners, work, 0)
    second_store = pltpu.make_async_copy(second, second_out, out_sem.at[1])
    second_store.start()

    def tail(c, carry):
        filled = valid_ref[me * cap + c] > 0
        stat = 0.95 * stats[c] + 0.05 / full_rows * gram[c]
        stats[c] = jnp.where(filled, stat, 0.0)
        power = dot(stat, bases[c], 1, 0, lax.Precision.HIGHEST)
        mean = jnp.sum(power * power, keepdims=True) / (full_cols * full_cols)
        iterate = power / (2.0 * jnp.sqrt(full_cols * mean + 1e-06))
        for sweep in range(2):
            iter_b = iterate.astype(BF16)
            square = dot(iter_b, iter_b, 0, 0).astype(BF16)
            iterate = 1.5 * iterate - 0.5 * dot(iter_b, square, 1, 0)
        bases[c] = jnp.where(filled, iterate, 0.0)
        return carry

    lax.fori_loop(0, cap, tail, 0)
    stats_store = pltpu.make_async_copy(stats, stats_out, out_sem.at[2])
    bases_store = pltpu.make_async_copy(bases, bases_out, out_sem.at[3])
    stats_store.start()
    bases_store.start()

    pltpu.make_async_copy(back, back, back_sem).wait()

    def place(j, carry):
        slot = slot_ref[j]
        update[j] = back[slot // cap, slot % cap]
        return carry

    lax.fori_loop(0, matrices, place, 0)
    update_store = pltpu.make_async_copy(update, update_out, out_sem.at[4])
    update_store.start()
    sent = send.at[pl.ds(0, devices - 1)]
    pltpu.make_async_copy(sent, sent, send_sem).wait()
    given = back.at[pl.ds(0, devices - 1)]
    pltpu.make_async_copy(given, given, step_sem).wait()
    for store in (newm_store, second_store, stats_store, bases_store, update_store):
        store.wait()


def local(gradients, moments, stats, bases, second, owner_list):
    matrices, rows, cols = gradients.shape
    cap, full_rows, full_cols = second.shape
    owners = lax.axis_size("owner")
    tensors = lax.axis_size("tensor")
    devices = owners * tensors
    matrix_ids = jnp.arange(matrices, dtype=jnp.int32)
    shared = owner_list[:, None] == owner_list[None, :]
    earlier = matrix_ids[:, None] < matrix_ids[None, :]
    position = jnp.sum((shared & earlier).astype(jnp.int32), axis=0)
    slot_id = owner_list * cap + position
    hit = jnp.arange(devices * cap, dtype=jnp.int32)[:, None] == slot_id[None, :]
    valid = jnp.sum(hit.astype(jnp.int32), axis=1)
    which = jnp.sum(jnp.where(hit, matrix_ids[None, :], 0), axis=1)

    hbm = pl.BlockSpec(memory_space=pl.ANY)
    smem = pl.BlockSpec(memory_space=pltpu.SMEM)
    second = second.reshape(cap, owners, rows, full_cols)
    like = lambda x: jax.ShapeDtypeStruct(x.shape, x.dtype)
    new_moments, update, new_stats, new_bases, new_second = pl.pallas_call(
        functools.partial(step_kernel, owners, tensors),
        out_shape=[like(moments), like(gradients), like(stats), like(bases), like(second)],
        in_specs=[smem] * 3 + [hbm] * 5,
        out_specs=[hbm] * 5,
        scratch_shapes=[
            pltpu.VMEM(gradients.shape, BF16),
            pltpu.VMEM(moments.shape, BF16),
            pltpu.VMEM(stats.shape, F32),
            pltpu.VMEM(bases.shape, F32),
            pltpu.VMEM(second.shape, BF16),
            pltpu.VMEM(bases.shape, BF16),
            pltpu.VMEM(stats.shape, F32),
            pltpu.VMEM((devices, cap, 2, rows, cols), BF16),
            pltpu.VMEM((owners, cap, 2, rows, full_cols), BF16),
            pltpu.VMEM((owners, cap, rows, full_cols), BF16),
            pltpu.VMEM((devices, cap, rows, cols), BF16),
            pltpu.VMEM(gradients.shape, BF16),
            pltpu.SemaphoreType.DMA((5,)),
            pltpu.SemaphoreType.DMA((5,)),
            pltpu.SemaphoreType.DMA,
            pltpu.SemaphoreType.DMA((owners,)),
            pltpu.SemaphoreType.DMA,
            pltpu.SemaphoreType.DMA,
        ],
        compiler_params=pltpu.CompilerParams(
            collective_id=0, has_side_effects=True, vmem_limit_bytes=56 * 1024 * 1024
        ),
    )(which, valid, slot_id, gradients, moments, stats, bases, second)
    return new_moments, update, new_stats, new_bases, new_second.reshape(cap, full_rows, full_cols)


def solution(mesh):
    dealt = P(None, "owner", "tensor")
    held = P(("owner", "tensor"), None, None)
    return jax.shard_map(
        local,
        mesh=mesh,
        in_specs=(dealt, dealt, held, held, held, P()),
        out_specs=(dealt, dealt, held, held, held),
        check_vma=False,
    )
```

```python
import functools

import jax
import jax.numpy as jnp
from jax import lax
from jax.experimental import pallas as pl
from jax.experimental.pallas import tpu as pltpu
from jax.sharding import PartitionSpec as P

MESH = pl.DeviceIdType.MESH
F32 = jnp.float32
BF16 = jnp.bfloat16
LEVELS = 4


def dot(a, b, ca, cb, precision=None):
    return lax.dot_general(
        a, b, (((ca,), (cb,)), ((), ())), precision=precision, preferred_element_type=F32
    )


def step_kernel(
    owners,
    tensors,
    room,
    first_ref,
    listed_ref,
    rank_ref,
    holder_ref,
    place_ref,
    valid_ref,
    grads_hbm,
    moms_hbm,
    stats_hbm,
    bases_hbm,
    second_hbm,
    newm_out,
    update_out,
    stats_out,
    bases_out,
    second_out,
    grads,
    moms,
    stats,
    bases,
    second,
    basis_b,
    gram,
    send,
    hop,
    transit,
    fan,
    got_first,
    got_second,
    steps_first,
    steps_second,
    gathered,
    hop_back,
    back,
    update,
    in_sem,
    out_sem,
    send_sem,
    got_sem,
):
    devices = owners * tensors
    matrices, rows, cols = grads.shape
    cap, full_cols = bases.shape[0], bases.shape[2]
    full_rows = owners * rows
    across = owners // LEVELS
    mates = across * tensors
    me_o, me_t = lax.axis_index("owner"), lax.axis_index("tensor")
    me = me_o * tensors + me_t
    level, column = me_o // across, me_o % across
    mate = column * tensors + me_t
    my_cols = pl.ds(pl.multiple_of(me_t * cols, cols), cols)
    first_sem, second_sem = got_sem.at[pl.ds(0, owners)], got_sem.at[pl.ds(owners, across)]
    hop_sem, gather_sem, back_sem, hop_back_sem = (got_sem.at[owners + across + i] for i in range(4))

    def shift(s):
        q = s % LEVELS
        by = jnp.where(q == 0, 2, jnp.where(q == 1, 1, jnp.where(q == 2, 3, 0)))
        return by, (s // LEVELS + 1) % across

    def target(s):
        by_level, by_column = shift(s)
        return ((level + by_level) % LEVELS) * across + (column + by_column) % across

    def source(s):
        by_level, by_column = shift(s)
        return (level - by_level + LEVELS) % LEVELS, (column - by_column + across) % across

    def remote(src, dst, sent, received, device):
        pltpu.make_async_remote_copy(
            src_ref=src,
            dst_ref=dst,
            send_sem=sent,
            recv_sem=received,
            device_id=device,
            device_id_type=MESH,
        ).start()

    def await_bytes(ref, sem):
        pltpu.make_async_copy(ref, ref, sem).wait()

    loads = [
        pltpu.make_async_copy(src, dst, in_sem.at[i])
        for i, (src, dst) in enumerate(
            (
                (grads_hbm, grads),
                (moms_hbm, moms),
                (bases_hbm, bases),
                (second_hbm, second),
                (stats_hbm, stats),
            )
        )
    ]
    for load in loads:
        load.start()

    barrier = pltpu.get_barrier_semaphore()

    def greet(k, carry):
        pl.semaphore_signal(
            barrier,
            inc=1,
            device_id=(target(k // tensors), (me_t + k % tensors + 1) % tensors),
            device_id_type=MESH,
        )
        return carry

    lax.fori_loop(0, devices - 1, greet, 0)
    loads[0].wait()
    loads[1].wait()

    def moment(j, carry):
        moms[j] = (0.9 * moms[j].astype(F32) + 0.1 * grads[j].astype(F32)).astype(BF16)
        return carry

    lax.fori_loop(0, matrices, moment, 0)
    pl.semaphore_wait(barrier, devices - 1)

    def leave(by):
        to = (level + by) % LEVELS

        def fill(p, carry):
            which = listed_ref[to * room + p]
            if by:
                hop[by - 1, p, 0] = grads[which]
                hop[by - 1, p, 1] = moms[which]
            else:
                transit[level, p, 0] = grads[which]
                transit[level, p, 1] = moms[which]
            return carry

        lax.fori_loop(0, room, fill, 0)
        if by:
            remote(
                hop.at[by - 1],
                transit.at[level],
                send_sem.at[0],
                hop_sem,
                (to * across + column, me_t),
            )

    for by in (2, 1, 3, 0):
        leave(by)

    def deal(k, carry):
        to, t = target(k // tensors), (me_t + k % tensors + 1) % tensors
        which = first_ref[to * tensors + t]
        send[k, 0] = grads[which]
        send[k, 1] = moms[which]

        @pl.when(k < devices - 1)
        def _():
            remote(
                send.at[k],
                got_first.at[level, column, :, :, my_cols],
                send_sem.at[1],
                first_sem.at[me_o],
                (to, t),
            )

        @pl.when(k == devices - 1)
        def _():
            pltpu.make_async_copy(
                send.at[k], got_first.at[level, column, :, :, my_cols], first_sem.at[me_o]
            ).start()

        return carry

    ahead = devices * 3 // 8
    lax.fori_loop(0, ahead, deal, 0)
    await_bytes(transit.at[pl.ds(0, LEVELS - 1)], hop_sem)

    def spread(k, carry):
        to = (mate + k + 1) % mates
        rank = rank_ref[level * mates + to]
        for a in range(LEVELS):
            fan[k, a] = transit[a, rank]

        @pl.when(k < mates - 1)
        def _():
            remote(
                fan.at[k],
                got_second.at[:, column, :, :, my_cols],
                send_sem.at[2],
                second_sem.at[column],
                (level * across + to // tensors, to % tensors),
            )

        @pl.when(k == mates - 1)
        def _():
            pltpu.make_async_copy(
                fan.at[k], got_second.at[:, column, :, :, my_cols], second_sem.at[column]
            ).start()

        return carry

    lax.fori_loop(0, mates, spread, 0)
    lax.fori_loop(ahead, devices, deal, 0)
    newm_store = pltpu.make_async_copy(moms, newm_out, out_sem.at[0])
    newm_store.start()

    for load in loads[2:]:
        load.wait()
    for c in range(cap):
        basis_b[c] = bases[c].astype(BF16)
        gram[c] = jnp.zeros((full_cols, full_cols), F32)

    def block(c, frm, grad, mom):
        basis = basis_b[c]
        gram[c] += dot(grad, grad, 0, 0)
        rotated = dot(grad, basis, 1, 0)
        following = 0.95 * second[c, frm].astype(F32) + 0.05 * rotated * rotated
        moment_rot = dot(mom, basis, 1, 0)
        scaled = (moment_rot / (jnp.sqrt(following) + 1e-06)).astype(BF16)
        filled = valid_ref[me * cap + c] > 0
        second[c, frm] = jnp.where(filled, following, 0.0).astype(BF16)
        return dot(scaled, basis, 1, 1).astype(BF16)

    def second_work(s, carry):
        x = (column + s + 1) % across
        await_bytes(got_second.at[:, x], second_sem.at[x])

        def one(a, carry):
            steps_second[s, a] = block(1, a * across + x, got_second[a, x, 0], got_second[a, x, 1])
            return carry

        lax.fori_loop(0, LEVELS, one, 0)

        def give(i, carry):
            t = (me_t + i + 1) % tensors
            piece = steps_second.at[s, :, :, pl.ds(pl.multiple_of(t * cols, cols), cols)]

            @pl.when(s * tensors + i < mates - 1)
            def _():
                remote(
                    piece, gathered.at[mate], send_sem.at[3], gather_sem, (level * across + x, t)
                )

            @pl.when(s * tensors + i == mates - 1)
            def _():
                pltpu.make_async_copy(piece, gathered.at[mate], gather_sem).start()

            return carry

        lax.fori_loop(0, tensors, give, 0)
        return carry

    lax.fori_loop(0, across, second_work, 0)

    def first_work(s, carry):
        z, x = source(s)
        frm = z * across + x
        await_bytes(got_first.at[z, x], first_sem.at[frm])
        steps_first[s] = block(0, frm, got_first[z, x, 0], got_first[z, x, 1])

        def give(i, carry):
            t = (me_t + i + 1) % tensors
            piece = steps_first.at[s, :, pl.ds(pl.multiple_of(t * cols, cols), cols)]

            @pl.when(s * tensors + i < devices - 1)
            def _():
                remote(piece, back.at[me], send_sem.at[4], back_sem, (frm, t))

            @pl.when(s * tensors + i == devices - 1)
            def _():
                pltpu.make_async_copy(piece, back.at[me], back_sem).start()

            return carry

        lax.fori_loop(0, tensors, give, 0)
        return carry

    lax.fori_loop(0, owners, first_work, 0)
    second_store = pltpu.make_async_copy(second, second_out, out_sem.at[1])
    second_store.start()

    await_bytes(gathered, gather_sem)
    mine = devices + level * room

    def home(by):
        to = (level + by) % LEVELS

        def fill(p, carry):
            piece = gathered[holder_ref[level * room + p], to]
            if by:
                hop_back[by - 1, p] = piece
            else:
                back[mine + p] = piece
            return carry

        lax.fori_loop(0, room, fill, 0)
        if by:
            remote(
                hop_back.at[by - 1],
                back.at[pl.ds(mine, room)],
                send_sem.at[5],
                hop_back_sem,
                (to * across + column, me_t),
            )

    for by in (2, 1, 3, 0):
        home(by)

    def tail(c, carry):
        filled = valid_ref[me * cap + c] > 0
        stat = 0.95 * stats[c] + 0.05 / full_rows * gram[c]
        stats[c] = jnp.where(filled, stat, 0.0)
        power = dot(stat, bases[c], 1, 0, lax.Precision.HIGHEST)
        mean = jnp.sum(power * power, keepdims=True) / (full_cols * full_cols)
        iterate = power / (2.0 * jnp.sqrt(full_cols * mean + 1e-06))
        for sweep in range(2):
            iter_b = iterate.astype(BF16)
            square = dot(iter_b, iter_b, 0, 0).astype(BF16)
            iterate = 1.5 * iterate - 0.5 * dot(iter_b, square, 1, 0)
        bases[c] = jnp.where(filled, iterate, 0.0)
        return carry

    lax.fori_loop(0, cap, tail, 0)
    stats_store = pltpu.make_async_copy(stats, stats_out, out_sem.at[2])
    bases_store = pltpu.make_async_copy(bases, bases_out, out_sem.at[3])
    stats_store.start()
    bases_store.start()

    await_bytes(back.at[pl.ds(0, devices)], back_sem)
    await_bytes(hop_back, hop_back_sem)

    def place(j, carry):
        update[j] = back[place_ref[j]]
        return carry

    lax.fori_loop(0, matrices, place, 0)
    update_store = pltpu.make_async_copy(update, update_out, out_sem.at[4])
    update_store.start()
    await_bytes(hop, send_sem.at[0])
    await_bytes(send.at[pl.ds(0, devices - 1)], send_sem.at[1])
    await_bytes(fan.at[pl.ds(0, mates - 1)], send_sem.at[2])
    await_bytes(gathered.at[pl.ds(0, mates - 1)], send_sem.at[3])
    await_bytes(back.at[pl.ds(0, devices - 1)], send_sem.at[4])
    await_bytes(hop_back, send_sem.at[5])
    for store in (newm_store, second_store, stats_store, bases_store, update_store):
        store.wait()


def local(gradients, moments, stats, bases, second, owner_list):
    matrices, rows, cols = gradients.shape
    cap, full_rows, full_cols = second.shape
    owners = lax.axis_size("owner")
    tensors = lax.axis_size("tensor")
    devices = owners * tensors
    across = owners // LEVELS
    mates = across * tensors
    i32 = jnp.int32
    matrix_ids = jnp.arange(matrices, dtype=i32)
    shared = owner_list[:, None] == owner_list[None, :]
    earlier = matrix_ids[:, None] < matrix_ids[None, :]
    position = jnp.sum((shared & earlier).astype(i32), axis=0)
    slot_id = owner_list * cap + position
    device_ids = jnp.arange(devices, dtype=i32)
    valid = jnp.sum(
        (jnp.arange(devices * cap, dtype=i32)[:, None] == slot_id[None, :]).astype(i32), axis=1
    )
    first = jnp.sum(
        jnp.where(device_ids[:, None] * cap == slot_id[None, :], matrix_ids[None, :], 0), axis=1
    )
    is_second = position == 1
    lower = is_second[None, :] & (owner_list[None, :] < device_ids[:, None])
    lower &= owner_list[None, :] // mates == device_ids[:, None] // mates
    rank = jnp.sum(lower.astype(i32), axis=1)
    fellow = is_second[:, None] & (owner_list[:, None] < owner_list[None, :])
    fellow &= owner_list[:, None] // mates == owner_list[None, :] // mates
    rank_of = jnp.sum(fellow.astype(i32), axis=0)
    level_of = owner_list // mates
    fullest = jnp.max(
        jnp.sum(
            (is_second[None, :] & (level_of[None, :] == jnp.arange(LEVELS, dtype=i32)[:, None])).astype(
                i32
            ),
            axis=1,
        )
    )

    hbm = pl.BlockSpec(memory_space=pl.ANY)
    smem = pl.BlockSpec(memory_space=pltpu.SMEM)
    second = second.reshape(cap, owners, rows, full_cols)
    like = lambda x: jax.ShapeDtypeStruct(x.shape, x.dtype)

    def step(collective, room, arrays):
        seats = jnp.arange(LEVELS * room, dtype=i32)
        hit = is_second[None, :] & (seats[:, None] == (level_of * room + rank_of)[None, :])
        listed = jnp.sum(jnp.where(hit, matrix_ids[None, :], 0), axis=1)
        holder = jnp.sum(jnp.where(hit, (owner_list % mates)[None, :], 0), axis=1)
        place = jnp.where(is_second, devices + level_of * room + rank_of, owner_list)
        return pl.pallas_call(
            functools.partial(step_kernel, owners, tensors, room),
            out_shape=[like(x) for x in (moments, gradients, stats, bases, second)],
            in_specs=[smem] * 6 + [hbm] * 5,
            out_specs=[hbm] * 5,
            scratch_shapes=[
                pltpu.VMEM(gradients.shape, BF16),
                pltpu.VMEM(moments.shape, BF16),
                pltpu.VMEM(stats.shape, F32),
                pltpu.VMEM(bases.shape, F32),
                pltpu.VMEM(second.shape, BF16),
                pltpu.VMEM(bases.shape, BF16),
                pltpu.VMEM(stats.shape, F32),
                pltpu.VMEM((devices, 2, rows, cols), BF16),
                pltpu.VMEM((LEVELS - 1, room, 2, rows, cols), BF16),
                pltpu.VMEM((LEVELS, room, 2, rows, cols), BF16),
                pltpu.VMEM((mates, LEVELS, 2, rows, cols), BF16),
                pltpu.VMEM((LEVELS, across, 2, rows, full_cols), BF16),
                pltpu.VMEM((LEVELS, across, 2, rows, full_cols), BF16),
                pltpu.VMEM((owners, rows, full_cols), BF16),
                pltpu.VMEM((across, LEVELS, rows, full_cols), BF16),
                pltpu.VMEM((mates, LEVELS, rows, cols), BF16),
                pltpu.VMEM((LEVELS - 1, room, rows, cols), BF16),
                pltpu.VMEM((devices + LEVELS * room, rows, cols), BF16),
                pltpu.VMEM(gradients.shape, BF16),
                pltpu.SemaphoreType.DMA((5,)),
                pltpu.SemaphoreType.DMA((5,)),
                pltpu.SemaphoreType.DMA((6,)),
                pltpu.SemaphoreType.DMA((owners + across + 4,)),
            ],
            compiler_params=pltpu.CompilerParams(
                collective_id=collective,
                has_side_effects=True,
                vmem_limit_bytes=58 * 1024 * 1024,
            ),
        )(first, listed, jnp.minimum(rank, room - 1), holder, place, valid, *arrays)

    rooms = (mates // 2, (5 * mates + 7) // 8, mates)
    pick = (fullest > rooms[0]).astype(i32) + (fullest > rooms[1]).astype(i32)
    new_moments, update, new_stats, new_bases, new_second = lax.switch(
        pick,
        [functools.partial(step, i, room) for i, room in enumerate(rooms)],
        (gradients, moments, stats, bases, second),
    )
    return new_moments, update, new_stats, new_bases, new_second.reshape(cap, full_rows, full_cols)


def solution(mesh):
    dealt = P(None, "owner", "tensor")
    held = P(("owner", "tensor"), None, None)
    return jax.shard_map(
        local,
        mesh=mesh,
        in_specs=(dealt, dealt, held, held, held, P()),
        out_specs=(dealt, dealt, held, held, held),
        check_vma=False,
    )
```

```python
import functools

import jax
import jax.numpy as jnp
from jax import lax
from jax.experimental import pallas as pl
from jax.experimental.pallas import tpu as pltpu
from jax.sharding import PartitionSpec as P

MESH = pl.DeviceIdType.MESH
F32 = jnp.float32
BF16 = jnp.bfloat16
LEVELS = 4


def dot(a, b, ca, cb, precision=None):
    return lax.dot_general(
        a, b, (((ca,), (cb,)), ((), ())), precision=precision, preferred_element_type=F32
    )


def step_kernel(
    owners,
    tensors,
    room,
    first_ref,
    listed_ref,
    rank_ref,
    holder_ref,
    count_ref,
    grads_hbm,
    moms_hbm,
    stats_hbm,
    bases_hbm,
    second_hbm,
    back,
    stats_out,
    bases_out,
    second_out,
    grads,
    moms,
    stats,
    bases,
    second,
    basis_b,
    gram,
    send,
    hop,
    transit,
    fan,
    got_first,
    got_second,
    steps_first,
    steps_second,
    gathered,
    hop_back,
    in_sem,
    out_sem,
    send_sem,
    got_sem,
):
    devices = owners * tensors
    _, rows, cols = grads.shape
    cap, full_cols = bases.shape[0], bases.shape[2]
    full_rows = owners * rows
    across = owners // LEVELS
    mates = across * tensors
    me_o, me_t = lax.axis_index("owner"), lax.axis_index("tensor")
    me = me_o * tensors + me_t
    level, column = me_o // across, me_o % across
    mate = column * tensors + me_t
    my_cols = pl.ds(pl.multiple_of(me_t * cols, cols), cols)
    first_sem, second_sem = got_sem.at[pl.ds(0, owners)], got_sem.at[pl.ds(owners, across)]
    hop_sem, gather_sem, back_sem, hop_back_sem = (got_sem.at[owners + across + i] for i in range(4))

    def shift(s):
        q = s % LEVELS
        by = jnp.where(q == 0, 2, jnp.where(q == 1, 1, jnp.where(q == 2, 3, 0)))
        return by, (s // LEVELS + 1) % across

    def target(s):
        by_level, by_column = shift(s)
        return ((level + by_level) % LEVELS) * across + (column + by_column) % across

    def source(s):
        by_level, by_column = shift(s)
        return (level - by_level + LEVELS) % LEVELS, (column - by_column + across) % across

    def remote(src, dst, sent, received, device):
        pltpu.make_async_remote_copy(
            src_ref=src,
            dst_ref=dst,
            send_sem=sent,
            recv_sem=received,
            device_id=device,
            device_id_type=MESH,
        ).start()

    def await_bytes(ref, sem):
        pltpu.make_async_copy(ref, ref, sem).wait()

    loads = [
        pltpu.make_async_copy(src, dst, in_sem.at[i])
        for i, (src, dst) in enumerate(
            (
                (grads_hbm, grads),
                (moms_hbm, moms),
                (bases_hbm, bases),
                (second_hbm, second),
                (stats_hbm, stats),
            )
        )
    ]
    for load in loads:
        load.start()

    barrier = pltpu.get_barrier_semaphore()

    def greet(k, carry):
        pl.semaphore_signal(
            barrier,
            inc=1,
            device_id=(target(k // tensors), (me_t + k % tensors + 1) % tensors),
            device_id_type=MESH,
        )
        return carry

    lax.fori_loop(0, devices - 1, greet, 0)
    loads[0].wait()
    loads[1].wait()

    pl.semaphore_wait(barrier, devices - 1)

    def leave(by):
        to = (level + by) % LEVELS

        def fill(p, carry):
            which = listed_ref[to * mates + p]
            if by:
                hop[by - 1, p, 0] = grads[which]
                hop[by - 1, p, 1] = moms[which]
            else:
                transit[level, p, 0] = grads[which]
                transit[level, p, 1] = moms[which]
            return carry

        lax.fori_loop(0, room, fill, 0)
        if by:
            remote(
                hop.at[by - 1],
                transit.at[level],
                send_sem.at[0],
                hop_sem,
                (to * across + column, me_t),
            )

    for by in (2, 1, 3, 0):
        leave(by)

    def deal(k, carry):
        to, t = target(k // tensors), (me_t + k % tensors + 1) % tensors
        which = first_ref[to * tensors + t]
        send[k, 0] = grads[which]
        send[k, 1] = moms[which]

        @pl.when(k < devices - 1)
        def _():
            remote(
                send.at[k],
                got_first.at[level, column, :, :, my_cols],
                send_sem.at[1],
                first_sem.at[me_o],
                (to, t),
            )

        @pl.when(k == devices - 1)
        def _():
            pltpu.make_async_copy(
                send.at[k], got_first.at[level, column, :, :, my_cols], first_sem.at[me_o]
            ).start()

        return carry

    ahead = devices * 3 // 8
    lax.fori_loop(0, ahead, deal, 0)
    await_bytes(transit.at[pl.ds(0, LEVELS - 1)], hop_sem)

    def spread(k, carry):
        to = (mate + k + 1) % mates
        rank = jnp.minimum(rank_ref[level * mates + to], room - 1)
        for a in range(LEVELS):
            fan[k, a] = transit[a, rank]

        @pl.when(k < mates - 1)
        def _():
            remote(
                fan.at[k],
                got_second.at[:, column, :, :, my_cols],
                send_sem.at[2],
                second_sem.at[column],
                (level * across + to // tensors, to % tensors),
            )

        @pl.when(k == mates - 1)
        def _():
            pltpu.make_async_copy(
                fan.at[k], got_second.at[:, column, :, :, my_cols], second_sem.at[column]
            ).start()

        return carry

    lax.fori_loop(0, mates, spread, 0)
    lax.fori_loop(ahead, devices, deal, 0)

    for load in loads[2:]:
        load.wait()
    for c in range(cap):
        basis_b[c] = bases[c].astype(BF16)
        gram[c] = jnp.zeros((full_cols, full_cols), F32)

    def block(c, frm, grad, mom):
        basis = basis_b[c]
        gram[c] += dot(grad, grad, 0, 0)
        rotated = dot(grad, basis, 1, 0)
        following = 0.95 * second[c, frm].astype(F32) + 0.05 * rotated * rotated
        moment_rot = dot(mom, basis, 1, 0)
        scaled = (moment_rot / (jnp.sqrt(following) + 1e-06)).astype(BF16)
        filled = count_ref[me] > c
        second[c, frm] = jnp.where(filled, following, 0.0).astype(BF16)
        return dot(scaled, basis, 1, 1).astype(BF16)

    def second_work(s, carry):
        x = (column + s + 1) % across
        await_bytes(got_second.at[:, x], second_sem.at[x])

        def one(a, carry):
            steps_second[s, a] = block(1, a * across + x, got_second[a, x, 0], got_second[a, x, 1])
            return carry

        lax.fori_loop(0, LEVELS, one, 0)

        def give(i, carry):
            t = (me_t + i + 1) % tensors
            piece = steps_second.at[s, :, :, pl.ds(pl.multiple_of(t * cols, cols), cols)]

            @pl.when(s * tensors + i < mates - 1)
            def _():
                remote(
                    piece, gathered.at[mate], send_sem.at[3], gather_sem, (level * across + x, t)
                )

            @pl.when(s * tensors + i == mates - 1)
            def _():
                pltpu.make_async_copy(piece, gathered.at[mate], gather_sem).start()

            return carry

        lax.fori_loop(0, tensors, give, 0)
        return carry

    def first_work(s, carry):
        z, x = source(s)
        frm = z * across + x
        await_bytes(got_first.at[z, x], first_sem.at[frm])
        steps_first[s] = block(0, frm, got_first[z, x, 0], got_first[z, x, 1])

        def give(i, carry):
            t = (me_t + i + 1) % tensors
            piece = steps_first.at[s, :, pl.ds(pl.multiple_of(t * cols, cols), cols)]

            @pl.when(s * tensors + i < devices - 1)
            def _():
                remote(piece, back.at[me], send_sem.at[4], back_sem, (frm, t))

            @pl.when(s * tensors + i == devices - 1)
            def _():
                pltpu.make_async_copy(piece, back.at[me], back_sem).start()

            return carry

        lax.fori_loop(0, tensors, give, 0)
        return carry

    early = owners * 3 // 8
    lax.fori_loop(0, early, first_work, 0)
    lax.fori_loop(0, across, second_work, 0)
    lax.fori_loop(early, owners, first_work, 0)
    second_store = pltpu.make_async_copy(second, second_out, out_sem.at[0])
    second_store.start()

    await_bytes(gathered, gather_sem)
    seats = back.at[pl.ds(devices + level * mates, room)]

    def home(by):
        to = (level + by) % LEVELS

        def fill(p, carry):
            hop_back[by, p] = gathered[holder_ref[level * mates + p], to]
            return carry

        lax.fori_loop(0, room, fill, 0)
        if by:
            remote(
                hop_back.at[by], seats, send_sem.at[5], hop_back_sem, (to * across + column, me_t)
            )
        else:
            pltpu.make_async_copy(hop_back.at[0], seats, hop_back_sem).start()

    for by in (2, 1, 3, 0):
        home(by)

    def tail(c, carry):
        filled = count_ref[me] > c
        stat = 0.95 * stats[c] + 0.05 / full_rows * gram[c]
        stats[c] = jnp.where(filled, stat, 0.0)
        power = dot(stat, bases[c], 1, 0, lax.Precision.HIGHEST)
        mean = jnp.sum(power * power, keepdims=True) / (full_cols * full_cols)
        iterate = power / (2.0 * jnp.sqrt(full_cols * mean + 1e-06))
        for sweep in range(2):
            iter_b = iterate.astype(BF16)
            square = dot(iter_b, iter_b, 0, 0).astype(BF16)
            iterate = 1.5 * iterate - 0.5 * dot(iter_b, square, 1, 0)
        bases[c] = jnp.where(filled, iterate, 0.0)
        return carry

    lax.fori_loop(0, cap, tail, 0)
    stats_store = pltpu.make_async_copy(stats, stats_out, out_sem.at[1])
    bases_store = pltpu.make_async_copy(bases, bases_out, out_sem.at[2])
    stats_store.start()
    bases_store.start()

    await_bytes(back.at[pl.ds(0, devices)], back_sem)
    await_bytes(hop_back, hop_back_sem)

    await_bytes(hop, send_sem.at[0])
    await_bytes(send.at[pl.ds(0, devices - 1)], send_sem.at[1])
    await_bytes(fan.at[pl.ds(0, mates - 1)], send_sem.at[2])
    await_bytes(gathered.at[pl.ds(0, mates - 1)], send_sem.at[3])
    await_bytes(back.at[pl.ds(0, devices - 1)], send_sem.at[4])
    await_bytes(hop_back.at[pl.ds(0, LEVELS - 1)], send_sem.at[5])
    for store in (second_store, stats_store, bases_store):
        store.wait()


def prepare_kernel(
    cap,
    mates,
    owner_ref,
    grads,
    moms,
    newm,
    first,
    listed,
    rank,
    holder,
    count,
    place,
    fullest,
    latter,
):
    matrices, devices = owner_ref.shape[0], first.shape[0]

    @pl.when(pl.program_id(0) == 0)
    def _():
        def clear(d, carry):
            for ref in (first, listed, holder, count, latter):
                ref[d] = 0
            return carry

        lax.fori_loop(0, devices, clear, 0)

        def enter(j, carry):
            owner = owner_ref[j]
            held = count[owner]
            place[j] = held
            first[owner] = jnp.where(held == 0, j, first[owner])
            latter[owner] = jnp.where(held == 1, j, latter[owner])
            count[owner] = held + 1
            return carry

        lax.fori_loop(0, matrices, enter, 0)

        most = 0
        for b in range(LEVELS):

            def number(i, seen):
                device = b * mates + i
                rank[device] = seen
                listed[b * mates + seen] = latter[device]
                holder[b * mates + seen] = i
                return seen + (count[device] > 1).astype(jnp.int32)

            most = jnp.maximum(most, lax.fori_loop(0, mates, number, jnp.int32(0)))
        fullest[0] = most

        def seat(j, carry):
            owner = owner_ref[j]
            shared = devices + owner // mates * mates + rank[owner]
            place[j] = jnp.where(place[j] == 0, owner, shared)
            return carry

        lax.fori_loop(0, matrices, seat, 0)

    newm[...] = (0.9 * moms[...].astype(F32) + 0.1 * grads[...].astype(F32)).astype(BF16)


def finish_kernel(place_ref, back, stats, bases, second, update, stats_out, bases_out, second_out, sem):
    matrices = update.shape[0]
    cap = stats.shape[0]
    whole = [
        pltpu.make_async_copy(src.at[c], dst.at[c], sem.at[matrices + i * cap + c])
        for c in range(cap)
        for i, (src, dst) in enumerate(
            ((second, second_out), (stats, stats_out), (bases, bases_out))
        )
    ]

    def piece(j):
        return pltpu.make_async_copy(back.at[place_ref[j]], update.at[j], sem.at[j])

    def start(j, carry):
        piece(j).start()
        return carry

    def wait(j, carry):
        piece(j).wait()
        return carry

    for copy in whole:
        copy.start()
    lax.fori_loop(0, matrices, start, 0)
    lax.fori_loop(0, matrices, wait, 0)
    for copy in whole:
        copy.wait()


def local(gradients, moments, stats, bases, second, owner_list):
    matrices, rows, cols = gradients.shape
    cap, full_rows, full_cols = second.shape
    owners = lax.axis_size("owner")
    tensors = lax.axis_size("tensor")
    devices = owners * tensors
    across = owners // LEVELS
    mates = across * tensors
    i32 = jnp.int32
    hbm = pl.BlockSpec(memory_space=pl.ANY)
    smem = pl.BlockSpec(memory_space=pltpu.SMEM)
    like = lambda x: jax.ShapeDtypeStruct(x.shape, x.dtype)
    ints = lambda n: jax.ShapeDtypeStruct((n,), i32)

    parts = 5 if matrices % 5 == 0 else 1
    block = pl.BlockSpec((matrices // parts, rows, cols), lambda i: (i, 0, 0))
    new_moments, first, listed, rank, holder, count, place, fullest = pl.pallas_call(
        functools.partial(prepare_kernel, cap, mates),
        grid=(parts,),
        out_shape=[like(moments)] + [ints(devices)] * 5 + [ints(matrices), ints(1)],
        in_specs=[smem, block, block],
        out_specs=[block] + [smem] * 7,
        scratch_shapes=[pltpu.SMEM((devices,), i32)],
    )(owner_list, gradients, moments)

    second = second.reshape(cap, owners, rows, full_cols)

    def step(collective, room, arrays):
        return pl.pallas_call(
            functools.partial(step_kernel, owners, tensors, room),
            out_shape=[
                jax.ShapeDtypeStruct((2 * devices, rows, cols), BF16),
                like(stats),
                like(bases),
                like(second),
            ],
            in_specs=[smem] * 5 + [hbm] * 5,
            out_specs=[hbm] * 4,
            scratch_shapes=[
                pltpu.VMEM(gradients.shape, BF16),
                pltpu.VMEM(moments.shape, BF16),
                pltpu.VMEM(stats.shape, F32),
                pltpu.VMEM(bases.shape, F32),
                pltpu.VMEM(second.shape, BF16),
                pltpu.VMEM(bases.shape, BF16),
                pltpu.VMEM(stats.shape, F32),
                pltpu.VMEM((devices, 2, rows, cols), BF16),
                pltpu.VMEM((LEVELS - 1, room, 2, rows, cols), BF16),
                pltpu.VMEM((LEVELS, room, 2, rows, cols), BF16),
                pltpu.VMEM((mates, LEVELS, 2, rows, cols), BF16),
                pltpu.VMEM((LEVELS, across, 2, rows, full_cols), BF16),
                pltpu.VMEM((LEVELS, across, 2, rows, full_cols), BF16),
                pltpu.VMEM((owners, rows, full_cols), BF16),
                pltpu.VMEM((across, LEVELS, rows, full_cols), BF16),
                pltpu.VMEM((mates, LEVELS, rows, cols), BF16),
                pltpu.VMEM((LEVELS, room, rows, cols), BF16),
                pltpu.SemaphoreType.DMA((5,)),
                pltpu.SemaphoreType.DMA((3,)),
                pltpu.SemaphoreType.DMA((6,)),
                pltpu.SemaphoreType.DMA((owners + across + 4,)),
            ],
            compiler_params=pltpu.CompilerParams(
                collective_id=collective,
                has_side_effects=True,
                vmem_limit_bytes=58 * 1024 * 1024,
            ),
        )(*arrays)

    rooms = [(mates * eighths + 7) // 8 for eighths in (3, 4, 5, 6, 8)]
    pick = sum((fullest[0] > room).astype(i32) for room in rooms[:-1])
    done = lax.switch(
        pick,
        [functools.partial(step, i, room) for i, room in enumerate(rooms)],
        (first, listed, rank, holder, count, gradients, new_moments, stats, bases, second),
    )
    update, new_stats, new_bases, new_second = pl.pallas_call(
        finish_kernel,
        out_shape=[like(gradients), like(stats), like(bases), like(second)],
        in_specs=[smem] + [hbm] * 4,
        out_specs=[hbm] * 4,
        scratch_shapes=[pltpu.SemaphoreType.DMA((matrices + 3 * cap,))],
    )(place, *done)
    return new_moments, update, new_stats, new_bases, new_second.reshape(cap, full_rows, full_cols)


def solution(mesh):
    dealt = P(None, "owner", "tensor")
    held = P(("owner", "tensor"), None, None)
    return jax.shard_map(
        local,
        mesh=mesh,
        in_specs=(dealt, dealt, held, held, held, P()),
        out_specs=(dealt, dealt, held, held, held),
        check_vma=False,
    )
```

```python
import functools

import jax
import jax.numpy as jnp
from jax import lax
from jax.experimental import pallas as pl
from jax.experimental.pallas import tpu as pltpu
from jax.sharding import PartitionSpec as P

MESH = pl.DeviceIdType.MESH
F32 = jnp.float32
BF16 = jnp.bfloat16
LEVELS = 4


def dot(a, b, ca, cb, precision=None):
    return lax.dot_general(
        a, b, (((ca,), (cb,)), ((), ())), precision=precision, preferred_element_type=F32
    )


def step_kernel(
    owners,
    tensors,
    room,
    first_ref,
    listed_ref,
    rank_ref,
    holder_ref,
    count_ref,
    grads_hbm,
    moms_hbm,
    stats_hbm,
    bases_hbm,
    second_hbm,
    back,
    stats_out,
    bases_out,
    second_out,
    grads,
    moms,
    stats,
    bases,
    second,
    basis_b,
    gram,
    send,
    hop,
    transit,
    fan,
    got_first,
    got_second,
    steps_first,
    steps_second,
    gathered,
    hop_back,
    in_sem,
    out_sem,
    send_sem,
    got_sem,
):
    devices = owners * tensors
    _, rows, cols = grads.shape
    cap, full_cols = bases.shape[0], bases.shape[2]
    full_rows = owners * rows
    across = owners // LEVELS
    mates = across * tensors
    me_o, me_t = lax.axis_index("owner"), lax.axis_index("tensor")
    me = me_o * tensors + me_t
    level, column = me_o // across, me_o % across
    mate = column * tensors + me_t
    my_cols = pl.ds(pl.multiple_of(me_t * cols, cols), cols)
    first_sem, second_sem = got_sem.at[pl.ds(0, owners)], got_sem.at[pl.ds(owners, across)]
    hop_sem, gather_sem, back_sem, hop_back_sem = (got_sem.at[owners + across + i] for i in range(4))

    def shift(s):
        q = s % LEVELS
        by = jnp.where(q == 0, 2, jnp.where(q == 1, 1, jnp.where(q == 2, 3, 0)))
        return by, (s // LEVELS + 1) % across

    def target(s):
        by_level, by_column = shift(s)
        return ((level + by_level) % LEVELS) * across + (column + by_column) % across

    def source(s):
        by_level, by_column = shift(s)
        return (level - by_level + LEVELS) % LEVELS, (column - by_column + across) % across

    def remote(src, dst, sent, received, device):
        pltpu.make_async_remote_copy(
            src_ref=src,
            dst_ref=dst,
            send_sem=sent,
            recv_sem=received,
            device_id=device,
            device_id_type=MESH,
        ).start()

    def await_bytes(ref, sem):
        pltpu.make_async_copy(ref, ref, sem).wait()

    loads = [
        pltpu.make_async_copy(src, dst, in_sem.at[i])
        for i, (src, dst) in enumerate(
            (
                (grads_hbm, grads),
                (moms_hbm, moms),
                (bases_hbm, bases),
                (second_hbm, second),
                (stats_hbm, stats),
            )
        )
    ]
    for load in loads:
        load.start()

    barrier = pltpu.get_barrier_semaphore()

    def greet(k, carry):
        pl.semaphore_signal(
            barrier,
            inc=1,
            device_id=(target(k // tensors), (me_t + k % tensors + 1) % tensors),
            device_id_type=MESH,
        )
        return carry

    lax.fori_loop(0, devices - 1, greet, 0)
    loads[0].wait()
    loads[1].wait()

    pl.semaphore_wait(barrier, devices - 1)

    def leave(by):
        to = (level + by) % LEVELS

        def fill(p, carry):
            which = listed_ref[to * mates + p]
            if by:
                hop[by - 1, p, 0] = grads[which]
                hop[by - 1, p, 1] = moms[which]
            else:
                transit[level, p, 0] = grads[which]
                transit[level, p, 1] = moms[which]
            return carry

        lax.fori_loop(0, room, fill, 0)
        if by:
            remote(
                hop.at[by - 1],
                transit.at[level],
                send_sem.at[0],
                hop_sem,
                (to * across + column, me_t),
            )

    for by in (2, 1, 3, 0):
        leave(by)

    def deal(k, carry):
        to, t = target(k // tensors), (me_t + k % tensors + 1) % tensors
        which = first_ref[to * tensors + t]
        send[k, 0] = grads[which]
        send[k, 1] = moms[which]

        @pl.when(k < devices - 1)
        def _():
            remote(
                send.at[k],
                got_first.at[level, column, :, :, my_cols],
                send_sem.at[1],
                first_sem.at[me_o],
                (to, t),
            )

        @pl.when(k == devices - 1)
        def _():
            pltpu.make_async_copy(
                send.at[k], got_first.at[level, column, :, :, my_cols], first_sem.at[me_o]
            ).start()

        return carry

    ahead = devices * 3 // 8
    lax.fori_loop(0, ahead, deal, 0)
    await_bytes(transit.at[pl.ds(0, LEVELS - 1)], hop_sem)

    def spread(k, carry):
        to = (mate + k + 1) % mates
        rank = jnp.minimum(rank_ref[level * mates + to], room - 1)
        for a in range(LEVELS):
            fan[k, a] = transit[a, rank]

        @pl.when(k < mates - 1)
        def _():
            remote(
                fan.at[k],
                got_second.at[:, column, :, :, my_cols],
                send_sem.at[2],
                second_sem.at[column],
                (level * across + to // tensors, to % tensors),
            )

        @pl.when(k == mates - 1)
        def _():
            pltpu.make_async_copy(
                fan.at[k], got_second.at[:, column, :, :, my_cols], second_sem.at[column]
            ).start()

        return carry

    lax.fori_loop(0, mates, spread, 0)
    lax.fori_loop(ahead, devices, deal, 0)

    for load in loads[2:]:
        load.wait()
    for c in range(cap):
        basis_b[c] = bases[c].astype(BF16)
        gram[c] = jnp.zeros((full_cols, full_cols), F32)

    def block(c, frm, grad, mom):
        basis = basis_b[c]
        gram[c] += dot(grad, grad, 0, 0)
        rotated = dot(grad, basis, 1, 0)
        following = 0.95 * second[c, frm].astype(F32) + 0.05 * rotated * rotated
        moment_rot = dot(mom, basis, 1, 0)
        scaled = (moment_rot / (jnp.sqrt(following) + 1e-06)).astype(BF16)
        filled = count_ref[me] > c
        second[c, frm] = jnp.where(filled, following, 0.0).astype(BF16)
        return dot(scaled, basis, 1, 1).astype(BF16)

    def second_work(s, carry):
        x = (column + s + 1) % across
        await_bytes(got_second.at[:, x], second_sem.at[x])

        def one(a, carry):
            steps_second[s, a] = block(1, a * across + x, got_second[a, x, 0], got_second[a, x, 1])
            return carry

        lax.fori_loop(0, LEVELS, one, 0)

        def give(i, carry):
            t = (me_t + i + 1) % tensors
            piece = steps_second.at[s, :, :, pl.ds(pl.multiple_of(t * cols, cols), cols)]

            @pl.when(s * tensors + i < mates - 1)
            def _():
                remote(
                    piece, gathered.at[mate], send_sem.at[3], gather_sem, (level * across + x, t)
                )

            @pl.when(s * tensors + i == mates - 1)
            def _():
                pltpu.make_async_copy(piece, gathered.at[mate], gather_sem).start()

            return carry

        lax.fori_loop(0, tensors, give, 0)
        return carry

    def first_work(s, carry):
        z, x = source(s)
        frm = z * across + x
        await_bytes(got_first.at[z, x], first_sem.at[frm])
        steps_first[s] = block(0, frm, got_first[z, x, 0], got_first[z, x, 1])

        def give(i, carry):
            t = (me_t + i + 1) % tensors
            piece = steps_first.at[s, :, pl.ds(pl.multiple_of(t * cols, cols), cols)]

            @pl.when(s * tensors + i < devices - 1)
            def _():
                remote(piece, back.at[me], send_sem.at[4], back_sem, (frm, t))

            @pl.when(s * tensors + i == devices - 1)
            def _():
                pltpu.make_async_copy(piece, back.at[me], back_sem).start()

            return carry

        lax.fori_loop(0, tensors, give, 0)
        return carry

    early = owners * 3 // 8
    lax.fori_loop(0, early, first_work, 0)
    lax.fori_loop(0, across, second_work, 0)
    lax.fori_loop(early, owners, first_work, 0)
    second_store = pltpu.make_async_copy(second, second_out, out_sem.at[0])
    second_store.start()

    await_bytes(gathered, gather_sem)
    seats = back.at[pl.ds(devices + level * mates, room)]

    def home(by):
        to = (level + by) % LEVELS

        def fill(p, carry):
            hop_back[by, p] = gathered[holder_ref[level * mates + p], to]
            return carry

        lax.fori_loop(0, room, fill, 0)
        if by:
            remote(
                hop_back.at[by], seats, send_sem.at[5], hop_back_sem, (to * across + column, me_t)
            )
        else:
            pltpu.make_async_copy(hop_back.at[0], seats, hop_back_sem).start()

    for by in (2, 1, 3, 0):
        home(by)

    def tail(c, carry):
        filled = count_ref[me] > c
        stat = 0.95 * stats[c] + 0.05 / full_rows * gram[c]
        stats[c] = jnp.where(filled, stat, 0.0)
        power = dot(stat, bases[c], 1, 0, lax.Precision.HIGHEST)
        mean = jnp.sum(power * power, keepdims=True) / (full_cols * full_cols)
        iterate = power / (2.0 * jnp.sqrt(full_cols * mean + 1e-06))
        for sweep in range(2):
            iter_b = iterate.astype(BF16)
            square = dot(iter_b, iter_b, 0, 0).astype(BF16)
            iterate = 1.5 * iterate - 0.5 * dot(iter_b, square, 1, 0)
        bases[c] = jnp.where(filled, iterate, 0.0)
        return carry

    lax.fori_loop(0, cap, tail, 0)
    stats_store = pltpu.make_async_copy(stats, stats_out, out_sem.at[1])
    bases_store = pltpu.make_async_copy(bases, bases_out, out_sem.at[2])
    stats_store.start()
    bases_store.start()

    await_bytes(back.at[pl.ds(0, devices)], back_sem)
    await_bytes(hop_back, hop_back_sem)

    await_bytes(hop, send_sem.at[0])
    await_bytes(send.at[pl.ds(0, devices - 1)], send_sem.at[1])
    await_bytes(fan.at[pl.ds(0, mates - 1)], send_sem.at[2])
    await_bytes(gathered.at[pl.ds(0, mates - 1)], send_sem.at[3])
    await_bytes(back.at[pl.ds(0, devices - 1)], send_sem.at[4])
    await_bytes(hop_back.at[pl.ds(0, LEVELS - 1)], send_sem.at[5])
    for store in (second_store, stats_store, bases_store):
        store.wait()


def prepare_kernel(
    cap,
    mates,
    owner_ref,
    grads,
    moms,
    newm,
    first,
    listed,
    rank,
    holder,
    count,
    place,
    fullest,
    latter,
):
    matrices, devices = owner_ref.shape[0], first.shape[0]

    @pl.when(pl.program_id(0) == 0)
    def _():
        def clear(d, carry):
            for ref in (first, listed, holder, count, latter):
                ref[d] = 0
            return carry

        lax.fori_loop(0, devices, clear, 0)

        def enter(j, carry):
            owner = owner_ref[j]
            held = count[owner]
            place[j] = held
            first[owner] = jnp.where(held == 0, j, first[owner])
            latter[owner] = jnp.where(held == 1, j, latter[owner])
            count[owner] = held + 1
            return carry

        lax.fori_loop(0, matrices, enter, 0)

        most = 0
        for b in range(LEVELS):

            def number(i, seen):
                device = b * mates + i
                rank[device] = seen
                listed[b * mates + seen] = latter[device]
                holder[b * mates + seen] = i
                return seen + (count[device] > 1).astype(jnp.int32)

            most = jnp.maximum(most, lax.fori_loop(0, mates, number, jnp.int32(0)))
        fullest[0] = most

        def seat(j, carry):
            owner = owner_ref[j]
            shared = devices + owner // mates * mates + rank[owner]
            place[j] = jnp.where(place[j] == 0, owner, shared)
            return carry

        lax.fori_loop(0, matrices, seat, 0)

    newm[...] = (0.9 * moms[...].astype(F32) + 0.1 * grads[...].astype(F32)).astype(BF16)


def finish_kernel(
    place_ref,
    back,
    stats,
    bases,
    second,
    update_out,
    stats_out,
    bases_out,
    second_out,
    update_held,
    stats_held,
    bases_held,
    second_held,
    in_sem,
    out_sem,
):
    matrices = update_held.shape[0]
    whole = [
        (
            pltpu.make_async_copy(src, held, in_sem.at[matrices + i]),
            pltpu.make_async_copy(held, dst, out_sem.at[i]),
        )
        for i, (src, held, dst) in enumerate(
            (
                (second, second_held, second_out),
                (stats, stats_held, stats_out),
                (bases, bases_held, bases_out),
            )
        )
    ]

    def piece(j):
        return pltpu.make_async_copy(back.at[place_ref[j]], update_held.at[j], in_sem.at[j])

    def start(j, carry):
        piece(j).start()
        return carry

    def wait(j, carry):
        piece(j).wait()
        return carry

    for load, _ in whole:
        load.start()
    lax.fori_loop(0, matrices, start, 0)
    for load, store in whole:
        load.wait()
        store.start()
    lax.fori_loop(0, matrices, wait, 0)
    placed = pltpu.make_async_copy(update_held, update_out, out_sem.at[3])
    placed.start()
    for _, store in whole:
        store.wait()
    placed.wait()


def local(gradients, moments, stats, bases, second, owner_list):
    matrices, rows, cols = gradients.shape
    cap, full_rows, full_cols = second.shape
    owners = lax.axis_size("owner")
    tensors = lax.axis_size("tensor")
    devices = owners * tensors
    across = owners // LEVELS
    mates = across * tensors
    i32 = jnp.int32
    hbm = pl.BlockSpec(memory_space=pl.ANY)
    smem = pl.BlockSpec(memory_space=pltpu.SMEM)
    like = lambda x: jax.ShapeDtypeStruct(x.shape, x.dtype)
    ints = lambda n: jax.ShapeDtypeStruct((n,), i32)

    parts = 5 if matrices % 5 == 0 else 1
    block = pl.BlockSpec((matrices // parts, rows, cols), lambda i: (i, 0, 0))
    new_moments, first, listed, rank, holder, count, place, fullest = pl.pallas_call(
        functools.partial(prepare_kernel, cap, mates),
        grid=(parts,),
        out_shape=[like(moments)] + [ints(devices)] * 5 + [ints(matrices), ints(1)],
        in_specs=[smem, block, block],
        out_specs=[block] + [smem] * 7,
        scratch_shapes=[pltpu.SMEM((devices,), i32)],
    )(owner_list, gradients, moments)

    second = second.reshape(cap, owners, rows, full_cols)

    def step(collective, room, arrays):
        return pl.pallas_call(
            functools.partial(step_kernel, owners, tensors, room),
            out_shape=[
                jax.ShapeDtypeStruct((2 * devices, rows, cols), BF16),
                like(stats),
                like(bases),
                like(second),
            ],
            in_specs=[smem] * 5 + [hbm] * 5,
            out_specs=[hbm] * 4,
            scratch_shapes=[
                pltpu.VMEM(gradients.shape, BF16),
                pltpu.VMEM(moments.shape, BF16),
                pltpu.VMEM(stats.shape, F32),
                pltpu.VMEM(bases.shape, F32),
                pltpu.VMEM(second.shape, BF16),
                pltpu.VMEM(bases.shape, BF16),
                pltpu.VMEM(stats.shape, F32),
                pltpu.VMEM((devices, 2, rows, cols), BF16),
                pltpu.VMEM((LEVELS - 1, room, 2, rows, cols), BF16),
                pltpu.VMEM((LEVELS, room, 2, rows, cols), BF16),
                pltpu.VMEM((mates, LEVELS, 2, rows, cols), BF16),
                pltpu.VMEM((LEVELS, across, 2, rows, full_cols), BF16),
                pltpu.VMEM((LEVELS, across, 2, rows, full_cols), BF16),
                pltpu.VMEM((owners, rows, full_cols), BF16),
                pltpu.VMEM((across, LEVELS, rows, full_cols), BF16),
                pltpu.VMEM((mates, LEVELS, rows, cols), BF16),
                pltpu.VMEM((LEVELS, room, rows, cols), BF16),
                pltpu.SemaphoreType.DMA((5,)),
                pltpu.SemaphoreType.DMA((3,)),
                pltpu.SemaphoreType.DMA((6,)),
                pltpu.SemaphoreType.DMA((owners + across + 4,)),
            ],
            compiler_params=pltpu.CompilerParams(
                collective_id=collective,
                has_side_effects=True,
                vmem_limit_bytes=58 * 1024 * 1024,
            ),
        )(*arrays)

    rooms = [(mates * eighths + 7) // 8 for eighths in (4, 5, 6, 8)]
    pick = sum((fullest[0] > room).astype(i32) for room in rooms[:-1])
    done = lax.switch(
        pick,
        [functools.partial(step, i, room) for i, room in enumerate(rooms)],
        (first, listed, rank, holder, count, gradients, new_moments, stats, bases, second),
    )
    update, new_stats, new_bases, new_second = pl.pallas_call(
        finish_kernel,
        out_shape=[like(gradients), like(stats), like(bases), like(second)],
        in_specs=[smem] + [hbm] * 4,
        out_specs=[hbm] * 4,
        scratch_shapes=[
            pltpu.VMEM(gradients.shape, BF16),
            pltpu.VMEM(stats.shape, F32),
            pltpu.VMEM(bases.shape, F32),
            pltpu.VMEM(second.shape, BF16),
            pltpu.SemaphoreType.DMA((matrices + 3,)),
            pltpu.SemaphoreType.DMA((4,)),
        ],
        compiler_params=pltpu.CompilerParams(vmem_limit_bytes=58 * 1024 * 1024),
    )(place, *done)
    return new_moments, update, new_stats, new_bases, new_second.reshape(cap, full_rows, full_cols)


def solution(mesh):
    dealt = P(None, "owner", "tensor")
    held = P(("owner", "tensor"), None, None)
    return jax.shard_map(
        local,
        mesh=mesh,
        in_specs=(dealt, dealt, held, held, held, P()),
        out_specs=(dealt, dealt, held, held, held),
        check_vma=False,
    )
```
